32 devices in a mesh: grp: 2 (over y), gx: 4 (over z), gy: 2 (over x), gz: 2 (over core).
Axes of the slice: x: 2, y: 2, z: 4, core: 2. Of those that a mesh axis runs over, the one named last changes fastest.
Arguments:
- voltages: int32 [1024, 49152], P('gy', ('grp', 'gx', 'gz')), parts along dimension 1, may hold values from -128 to 127
Outputs:
- visibilities: bfloat16 [256, 2, 1024, 1024], P(('grp', 'gx', 'gz'), None, 'gy'), parts along dimension 0
The draws below stay inside these ranges and needn't reach their ends.
There are 2 independent parts, one for each index of `grp`. The reference program is written for one: setup_inputs(seed, part) draws one part's arguments, and reference() takes and returns one part's arrays. A program takes and returns all parts, laid end to end along the dimension named above; each array names one. Nothing has to cross between parts.
All inputs are finite; a program needn't handle non-finite values.
Results may differ from the reference program's by a relative error of at most 0.0056.
Values may be sent and summed in bfloat16 or wider, within the bound.
A program may use at most 128 MiB of HBM per device.

```python
import math
import jax
import jax.numpy as jnp
from jax import lax

INPUTS = 1024
CHANS = 128
POINTS = 512
TAPS = 4
NSPEC = 48
SAMPLES = 24576


def draw_voltages(key, part):
    key = jax.random.fold_in(key, 7)
    key_sky, key_delay, key_noise = jax.random.split(key, 3)
    sky = jax.random.randint(key_sky, (SAMPLES + 64,), -48, 49)
    delays = jax.random.randint(key_delay, (INPUTS, 1), 0, 64)
    places = delays + jnp.arange(SAMPLES, dtype=jnp.int32)[None, :]
    noise = jax.random.randint(key_noise, (INPUTS, SAMPLES), -80, 81)
    return jnp.clip(sky[places] + noise, -128, 127).astype(jnp.int32)


def setup_inputs(seed: int = 0, part: int = 0) -> dict:
    streams_of = jax.random.split(jax.random.key(seed), 2)
    part_keys = jax.random.split(jax.random.fold_in(streams_of[1], part), 2)
    voltages = draw_voltages(jax.random.fold_in(jax.random.fold_in(streams_of[1], part), 71), part)
    return {"voltages": voltages}


def filter_taps(taps_count, points):
    index = jnp.arange(taps_count * points, dtype=jnp.float32)
    centre = (taps_count * points - 1) / 2.0
    window = 0.5 - 0.5 * jnp.cos(2.0 * math.pi * (index + 0.5) / (taps_count * points))
    return (jnp.sinc((index - centre) / points) * window).astype(jnp.float32).reshape(taps_count, points)

def basis_table(channels, points):
    sample = jnp.arange(points, dtype=jnp.int32)[None, :]
    channel = 64 + jnp.arange(channels, dtype=jnp.int32)[:, None]
    phase = (sample * channel % points).astype(jnp.float32) * (2.0 * math.pi / points)
    scale = 1.0 / math.sqrt(points)
    return jnp.stack([jnp.cos(phase) * scale, -jnp.sin(phase) * scale], axis=1).astype(jnp.bfloat16)

def reference(voltages):
    taps = filter_taps(TAPS, POINTS)
    blocks = voltages.astype(jnp.float32).reshape(INPUTS, NSPEC, POINTS)
    padded = jnp.concatenate([jnp.zeros((INPUTS, TAPS - 1, POINTS), jnp.float32), blocks], axis=1)
    running = jnp.zeros((INPUTS, NSPEC, POINTS), jnp.float32)
    for offset in range(TAPS):
        running = running + taps[offset][None, None, :] * padded[:, offset:offset + NSPEC]
    frames = (running * (1.0 / 128.0)).astype(jnp.bfloat16)
    basis = basis_table(CHANS, POINTS)
    flat_basis = basis.reshape(CHANS * 2, POINTS).T
    spectra = jnp.dot(frames.reshape(INPUTS * NSPEC, POINTS), flat_basis, preferred_element_type=jnp.float32)
    spectra = spectra.astype(jnp.bfloat16).reshape(INPUTS, NSPEC, CHANS, 2)
    spectra = jnp.transpose(spectra, (2, 0, 1, 3))

    def correlate(single):
        real_part = single[:, :, 0]
        imag_part = single[:, :, 1]
        rows_a = jnp.concatenate([real_part, imag_part], axis=1)
        rows_b = jnp.concatenate([imag_part, -real_part], axis=1)
        real_out = jnp.dot(rows_a, rows_a.T, preferred_element_type=jnp.float32)
        imag_out = jnp.dot(rows_b, rows_a.T, preferred_element_type=jnp.float32)
        both = jnp.stack([real_out, imag_out], axis=0) * (1.0 / NSPEC)
        return both.astype(jnp.bfloat16)
    return lax.map(correlate, spectra)
```

```python
import functools
import math

import jax
import jax.numpy as jnp
import numpy as np
from jax import lax
from jax.experimental import pallas as pl
from jax.experimental.pallas import tpu as pltpu
from jax.sharding import PartitionSpec as P

CHANS = 128
POINTS = 512
TAPS = 4
LANES = 128
MESH = pl.DeviceIdType.MESH
F32 = jnp.float32
BF16 = jnp.bfloat16


def filter_taps():
    index = np.arange(TAPS * POINTS, dtype=np.float64)
    centre = (TAPS * POINTS - 1) / 2.0
    window = 0.5 - 0.5 * np.cos(2.0 * math.pi * (index + 0.5) / (TAPS * POINTS))
    taps = (np.sinc((index - centre) / POINTS) * window).astype(np.float32)
    return (taps / np.float32(128.0)).reshape(TAPS, POINTS)


def basis_rows(peers, rows_per):
    sample = np.arange(POINTS)[None, :]
    channel = 64 + np.arange(CHANS)[:, None]
    phase = (sample * channel % POINTS) * (2.0 * math.pi / POINTS)
    scale = 1.0 / math.sqrt(POINTS)
    table = np.stack([np.cos(phase) * scale, -np.sin(phase) * scale], axis=1)
    table = table.reshape(peers, -1, POINTS)
    out = np.zeros((peers, rows_per, POINTS), np.float32)
    out[:, : table.shape[1]] = table
    return out.reshape(peers * rows_per, POINTS)


def spread_kernel(
    gxn, gzn, gyn, spec, rows_per,
    v_ref, taps_ref, basis_ref, g_ref,
    frames, spectra, tail_out, tail_in,
    send_sem, recv_sem, pass_send, pass_recv, local_sem, tail_sem,
):
    peers = gxn * gzn
    inputs = v_ref.shape[0]
    x = lax.axis_index("gy")
    me = lax.axis_index("gx") * gzn + lax.axis_index("gz")

    def at(peer):
        return {"gx": peer // gzn, "gz": lax.rem(peer, gzn)}

    def across(k):
        return {"gy": lax.rem(x + k, gyn)}

    barrier = pltpu.get_barrier_semaphore()

    def greet(k, carry):
        pl.semaphore_signal(
            barrier, inc=1, device_id=at(lax.rem(me + k, peers)), device_id_type=MESH
        )
        return carry

    lax.fori_loop(1, peers, greet, 0)
    for k in range(1, gyn):
        pl.semaphore_signal(barrier, inc=1, device_id=across(k), device_id_type=MESH)

    step = 32

    def filtered(slot, terms):
        def body(chunk, carry):
            rows = pl.ds(pl.multiple_of(chunk * step, step), step)
            total = jnp.zeros((step, POINTS), F32)
            for tap, block in terms:
                piece = v_ref[rows, block * POINTS : (block + 1) * POINTS].astype(F32)
                total = total + taps_ref[tap : tap + 1, :] * piece
            frames[slot, rows, :] = total.astype(BF16)
            return carry

        lax.fori_loop(0, inputs // step, body, 0)
        return lax.dot_general(
            basis_ref[...], frames[slot], (((1,), (1,)), ((), ())), preferred_element_type=F32
        )

    def rows_of(peer, s):
        return pl.ds(pl.multiple_of((peer * spec + s) * rows_per, rows_per), rows_per)

    def owned(peer):
        return pl.ds(pl.multiple_of(peer * rows_per, rows_per), rows_per)

    def send(peer, s):
        return pltpu.make_async_remote_copy(
            src_ref=spectra.at[s, owned(peer)],
            dst_ref=g_ref.at[x, rows_of(me, s)],
            send_sem=send_sem.at[peer, s],
            recv_sem=recv_sem.at[me, s],
            device_id=at(peer),
            device_id_type=MESH,
        )

    def arrival(peer, s):
        return pltpu.make_async_remote_copy(
            src_ref=spectra.at[s, owned(peer)],
            dst_ref=g_ref.at[x, rows_of(peer, s)],
            send_sem=send_sem.at[peer, s],
            recv_sem=recv_sem.at[peer, s],
            device_id=at(peer),
            device_id_type=MESH,
        )

    def pass_on(source, peer, s, k):
        return pltpu.make_async_remote_copy(
            src_ref=source,
            dst_ref=g_ref.at[x, rows_of(peer, s)],
            send_sem=pass_send.at[k - 1, peer, s],
            recv_sem=pass_recv.at[k - 1, peer, s],
            device_id=across(k),
            device_id_type=MESH,
        )

    def passed(peer, s, k):
        y = lax.rem(x - k + gyn, gyn)
        return pltpu.make_async_remote_copy(
            src_ref=g_ref.at[y, rows_of(peer, s)],
            dst_ref=g_ref.at[y, rows_of(peer, s)],
            send_sem=pass_send.at[k - 1, peer, s],
            recv_sem=pass_recv.at[k - 1, peer, s],
            device_id=across(k),
            device_id_type=MESH,
        )

    def local(s):
        return pltpu.make_async_copy(
            spectra.at[s, owned(me)], g_ref.at[x, rows_of(me, s)], local_sem.at[s]
        )

    def tail(peer):
        return pltpu.make_async_remote_copy(
            src_ref=tail_out,
            dst_ref=tail_in,
            send_sem=tail_sem.at[0],
            recv_sem=tail_sem.at[1],
            device_id=at(peer),
            device_id_type=MESH,
        )

    for s in range(TAPS - 1):
        terms = [(t, spec + s - 3 + t) for t in range(TAPS) if s - 3 + t < 0]
        tail_out[s] = filtered(s % 2, terms).astype(BF16)

    pl.semaphore_wait(barrier, peers - 1 + gyn - 1)

    @pl.when(me < peers - 1)
    def _():
        tail(me + 1).start()

    def launch(s):
        local(s).start()
        for k in range(1, gyn):
            pass_on(spectra.at[s, owned(me)], me, s, k).start()

        def body(k, carry):
            send(lax.rem(me + peers - k, peers), s).start()
            return carry

        lax.fori_loop(1, peers, body, 0)

    order = list(range(TAPS - 1, spec)) + list(range(TAPS - 1))
    for s in order:
        terms = [(t, s - 3 + t) for t in range(TAPS) if s - 3 + t >= 0]
        found = filtered(s % 2, terms)
        if s < TAPS - 1:
            if s == 0:
                @pl.when(me > 0)
                def _():
                    tail(me - 1).wait_recv()

                @pl.when(me == 0)
                def _():
                    tail_in[...] = jnp.zeros_like(tail_in)

            found = found + tail_in[s].astype(F32)
        spectra[s] = found.astype(BF16)
        launch(s)

    for s in order:
        def body(k, carry, s=s):
            peer = lax.rem(me + k, peers)
            arrival(peer, s).wait_recv()
            for j in range(1, gyn):
                pass_on(g_ref.at[x, rows_of(peer, s)], peer, s, j).start()
            return carry

        lax.fori_loop(1, peers, body, 0)

    @pl.when(me < peers - 1)
    def _():
        tail(me + 1).wait_send()

    for s in order:
        local(s).wait()

        def body(k, carry, s=s):
            send(lax.rem(me + k, peers), s).wait_send()
            return carry

        lax.fori_loop(1, peers, body, 0)

        def body(peer, carry, s=s):
            for j in range(1, gyn):
                passed(peer, s, j).wait()
            return carry

        lax.fori_loop(0, peers, body, 0)


def correlate_kernel(gyn, times, rows_per, rows_kept, inverse, g_ref, out_ref, wide, right):
    x = lax.axis_index("gy")
    c = pl.program_id(0)
    inputs = g_ref.shape[2]
    depth = right.shape[0]

    @pl.when(c == 0)
    def _():
        right[...] = jnp.zeros_like(right)
        for y in range(gyn):
            def body(t, carry, y=y):
                source = pl.ds(pl.multiple_of(t * rows_per, rows_per), rows_per)
                target = pl.ds(pl.multiple_of(t * rows_kept, rows_kept), rows_kept)
                block = g_ref[y, source, :].astype(F32)[:rows_kept]
                for lane in range(inputs // LANES):
                    wide[y, lane, target, :] = block[:, lane * LANES : (lane + 1) * LANES]
                return carry

            lax.fori_loop(0, times, body, 0)

    def part(y, r):
        rows = pl.ds(2 * c + r, times, rows_kept)
        return jnp.concatenate(
            [wide[y, lane, rows, :] for lane in range(inputs // LANES)], axis=1
        )

    for y in range(gyn):
        real, imag = part(y, 0), part(y, 1)
        left, far = slice(y * inputs, (y + 1) * inputs), slice(
            (gyn + y) * inputs, (gyn + y + 1) * inputs
        )
        right[0:times, left] = real.astype(BF16)
        right[times : 2 * times, left] = imag.astype(BF16)
        right[0:times, far] = (-imag).astype(BF16)
        right[times : 2 * times, far] = real.astype(BF16)

    pieces = [part(x, 0), part(x, 1)]
    if depth > 2 * times:
        pieces.append(jnp.zeros((depth - 2 * times, inputs), F32))
    turned = jnp.transpose(jnp.concatenate(pieces, axis=0)).astype(BF16)
    for r in range(2):
        for y in range(gyn):
            left = slice((r * gyn + y) * inputs, (r * gyn + y + 1) * inputs)
            product = jnp.dot(turned, right[:, left], preferred_element_type=F32)
            out_ref[0, r, :, y * inputs : (y + 1) * inputs] = (product * inverse).astype(BF16)


def solution(mesh):
    gxn, gzn, gyn = mesh.shape["gx"], mesh.shape["gz"], mesh.shape["gy"]
    peers = gxn * gzn
    chans = CHANS // peers
    rows_per = -(-2 * chans // 16) * 16
    rows_kept = -(-2 * chans // 8) * 8
    taps = filter_taps()
    basis = basis_rows(peers, rows_per)

    def per_device(voltages):
        inputs = voltages.shape[0]
        spec = voltages.shape[1] // POINTS
        times = spec * peers
        vmem = pl.BlockSpec(memory_space=pltpu.VMEM)
        dma = pltpu.SemaphoreType.DMA
        gathered = pl.pallas_call(
            functools.partial(spread_kernel, gxn, gzn, gyn, spec, rows_per),
            out_shape=jax.ShapeDtypeStruct((gyn, times * rows_per, inputs), BF16),
            in_specs=[vmem] * 3,
            out_specs=pl.BlockSpec(memory_space=pl.ANY),
            scratch_shapes=[
                pltpu.VMEM((2, inputs, POINTS), BF16),
                pltpu.VMEM((spec, peers * rows_per, inputs), BF16),
                pltpu.VMEM((TAPS - 1, peers * rows_per, inputs), BF16),
                pltpu.VMEM((TAPS - 1, peers * rows_per, inputs), BF16),
                dma((peers, spec)),
                dma((peers, spec)),
                dma((gyn - 1, peers, spec)),
                dma((gyn - 1, peers, spec)),
                dma((spec,)),
                dma((2,)),
            ],
            compiler_params=pltpu.CompilerParams(
                collective_id=0, has_side_effects=True, vmem_limit_bytes=48 * 2**20
            ),
        )(voltages, jnp.asarray(taps), jnp.asarray(basis, BF16))
        depth = -(-2 * times // 128) * 128
        return pl.pallas_call(
            functools.partial(
                correlate_kernel, gyn, times, rows_per, rows_kept, 1.0 / times
            ),
            grid=(chans,),
            out_shape=jax.ShapeDtypeStruct((chans, 2, inputs, gyn * inputs), BF16),
            in_specs=[
                pl.BlockSpec(
                    (gyn, times * rows_per, inputs),
                    lambda c: (0, 0, 0),
                    pipeline_mode=pl.Buffered(1),
                )
            ],
            out_specs=pl.BlockSpec((1, 2, inputs, gyn * inputs), lambda c: (c, 0, 0, 0)),
            scratch_shapes=[
                pltpu.VMEM((gyn, inputs // LANES, times * rows_kept, LANES), F32),
                pltpu.VMEM((depth, 2 * gyn * inputs), BF16),
            ],
            compiler_params=pltpu.CompilerParams(
                dimension_semantics=("arbitrary",), vmem_limit_bytes=56 * 2**20
            ),
        )(gathered)

    return jax.shard_map(
        per_device,
        mesh=mesh,
        in_specs=(P("gy", ("grp", "gx", "gz")),),
        out_specs=P(("grp", "gx", "gz"), None, "gy", None),
        check_vma=False,
    )
```

```python
import functools
import math

import jax
import jax.numpy as jnp
import numpy as np
from jax import lax
from jax.experimental import pallas as pl
from jax.experimental.pallas import tpu as pltpu
from jax.sharding import PartitionSpec as P

CHANS = 128
POINTS = 512
TAPS = 4
LANES = 128
LOADS = 4
STEP = 16
AHEAD = 5
CUTS = 4
NB = 256
PER = 2
MESH = pl.DeviceIdType.MESH
F32 = jnp.float32
BF16 = jnp.bfloat16


def filter_taps():
    index = np.arange(TAPS * POINTS, dtype=np.float64)
    centre = (TAPS * POINTS - 1) / 2.0
    window = 0.5 - 0.5 * np.cos(2.0 * math.pi * (index + 0.5) / (TAPS * POINTS))
    taps = (np.sinc((index - centre) / POINTS) * window).astype(np.float32)
    return (taps / np.float32(128.0)).reshape(TAPS, POINTS)


def basis_rows(peers, rows_per):
    sample = np.arange(POINTS)[None, :]
    channel = 64 + np.arange(CHANS)[:, None]
    phase = (sample * channel % POINTS) * (2.0 * math.pi / POINTS)
    scale = 1.0 / math.sqrt(POINTS)
    table = np.stack([np.cos(phase) * scale, -np.sin(phase) * scale], axis=1)
    table = table.reshape(peers, -1, POINTS)
    out = np.zeros((peers, rows_per, POINTS), np.float32)
    out[:, : table.shape[1]] = table
    return out.reshape(peers * rows_per, POINTS)


def spread_kernel(
    gxn, gzn, gyn, spec, rows_per,
    v_ref, taps_ref, basis_ref, g_ref,
    samples, taps, basis, frames, spectra, tail_out, tail_in, load_sem,
    send_sem, recv_sem, pass_send, pass_recv, local_sem, tail_sem,
):
    peers = gxn * gzn
    inputs = v_ref.shape[0]
    x = lax.axis_index("gy")
    me = lax.axis_index("gx") * gzn + lax.axis_index("gz")

    def at(peer):
        return {"gx": peer // gzn, "gz": lax.rem(peer, gzn)}

    def across(k):
        return {"gy": lax.rem(x + k, gyn)}

    barrier = pltpu.get_barrier_semaphore()

    def greet(k, carry):
        pl.semaphore_signal(
            barrier, inc=1, device_id=at(lax.rem(me + k, peers)), device_id_type=MESH
        )
        return carry

    lax.fori_loop(1, peers, greet, 0)
    for k in range(1, gyn):
        pl.semaphore_signal(barrier, inc=1, device_id=across(k), device_id_type=MESH)

    chunk = inputs // LOADS

    def loading(j):
        rows = slice(j * chunk, (j + 1) * chunk)
        return pltpu.make_async_copy(v_ref.at[rows], samples.at[rows], load_sem.at[j])

    loads = [
        pltpu.make_async_copy(taps_ref, taps, load_sem.at[LOADS]),
        pltpu.make_async_copy(basis_ref, basis, load_sem.at[LOADS + 1]),
    ]
    loads[0].start()
    for j in range(LOADS):
        loading(j).start()
    loads[1].start()
    loads[0].wait()

    shares = [
        [(t, s - 3 + t) for t in range(TAPS) if 0 <= s - 3 + t < spec]
        for s in range(spec + TAPS - 1)
    ]
    for j in range(LOADS):
        loading(j).wait()
        for lane in range(POINTS // LANES):
            lanes = slice(lane * LANES, (lane + 1) * LANES)
            held = [
                jnp.broadcast_to(taps[t : t + 1, lanes], (STEP, LANES)) for t in range(TAPS)
            ]

            def body(i, carry, j=j, lane=lane, lanes=lanes, held=held):
                rows = pl.ds(pl.multiple_of(j * chunk + i * STEP, STEP), STEP)
                pieces = [
                    samples[rows, b * POINTS + lane * LANES : b * POINTS + (lane + 1) * LANES]
                    .astype(F32)
                    for b in range(spec)
                ]
                for s, terms in enumerate(shares):
                    total = None
                    for t, b in terms:
                        term = held[t] * pieces[b]
                        total = term if total is None else total + term
                    frames[s, rows, lanes] = total.astype(BF16)
                return carry

            lax.fori_loop(0, chunk // STEP, body, 0, unroll=2)
    loads[1].wait()

    def transformed(s):
        return lax.dot_general(
            basis[...], frames[s], (((1,), (1,)), ((), ())), preferred_element_type=F32
        )

    def rows_of(peer, s):
        return pl.ds(pl.multiple_of((peer * spec + s) * rows_per, rows_per), rows_per)

    def owned(peer):
        return pl.ds(pl.multiple_of(peer * rows_per, rows_per), rows_per)

    def send(peer, s):
        return pltpu.make_async_remote_copy(
            src_ref=spectra.at[s, owned(peer)],
            dst_ref=g_ref.at[x, rows_of(me, s)],
            send_sem=send_sem.at[peer, s],
            recv_sem=recv_sem.at[me, s],
            device_id=at(peer),
            device_id_type=MESH,
        )

    def arrival(peer, s):
        return pltpu.make_async_remote_copy(
            src_ref=spectra.at[s, owned(peer)],
            dst_ref=g_ref.at[x, rows_of(peer, s)],
            send_sem=send_sem.at[peer, s],
            recv_sem=recv_sem.at[peer, s],
            device_id=at(peer),
            device_id_type=MESH,
        )

    def pass_on(source, peer, s, k):
        return pltpu.make_async_remote_copy(
            src_ref=source,
            dst_ref=g_ref.at[x, rows_of(peer, s)],
            send_sem=pass_send.at[k - 1, peer, s],
            recv_sem=pass_recv.at[k - 1, peer, s],
            device_id=across(k),
            device_id_type=MESH,
        )

    def passed(peer, s, k):
        y = lax.rem(x - k + gyn, gyn)
        return pltpu.make_async_remote_copy(
            src_ref=g_ref.at[y, rows_of(peer, s)],
            dst_ref=g_ref.at[y, rows_of(peer, s)],
            send_sem=pass_send.at[k - 1, peer, s],
            recv_sem=pass_recv.at[k - 1, peer, s],
            device_id=across(k),
            device_id_type=MESH,
        )

    def local(s):
        return pltpu.make_async_copy(
            spectra.at[s, owned(me)], g_ref.at[x, rows_of(me, s)], local_sem.at[s]
        )

    cut = tail_out.shape[1] // CUTS

    def tail(peer, s):
        return [
            pltpu.make_async_remote_copy(
                src_ref=tail_out.at[s, pl.ds(q * cut, cut)],
                dst_ref=tail_in.at[s, pl.ds(q * cut, cut)],
                send_sem=tail_sem.at[0, s, q],
                recv_sem=tail_sem.at[1, s, q],
                device_id=at(peer),
                device_id_type=MESH,
            )
            for q in range(CUTS)
        ]

    for s in range(TAPS - 1):
        tail_out[s] = transformed(spec + s).astype(BF16)
        if s == 0:
            pl.semaphore_wait(barrier, peers - 1 + gyn - 1)

        @pl.when(me < peers - 1)
        def _(s=s):
            for copy in tail(me + 1, s):
                copy.start()

    def launch(s):
        local(s).start()
        for k in range(1, gyn):
            pass_on(spectra.at[s, owned(me)], me, s, k).start()

        def body(k, carry):
            send(lax.rem(me + peers - k, peers), s).start()
            return carry

        lax.fori_loop(1, peers, body, 0)

    order = list(range(spec))

    def produce(s):
        found = transformed(s)
        if s < TAPS - 1:
            @pl.when(me > 0)
            def _():
                for copy in tail(me - 1, s):
                    copy.wait_recv()

            @pl.when(me == 0)
            def _():
                tail_in[s] = jnp.zeros_like(tail_in[s])

            found = found + tail_in[s].astype(F32)
        spectra[s] = found.astype(BF16)
        launch(s)

    def relay(s):
        def body(k, carry):
            peer = lax.rem(me + k, peers)
            arrival(peer, s).wait_recv()
            for j in range(1, gyn):
                pass_on(g_ref.at[x, rows_of(peer, s)], peer, s, j).start()
            return carry

        lax.fori_loop(1, peers, body, 0)

    for i in range(spec + AHEAD):
        if i < spec:
            produce(order[i])
        if i >= AHEAD:
            relay(order[i - AHEAD])

    @pl.when(me < peers - 1)
    def _():
        for s in range(TAPS - 1):
            for copy in tail(me + 1, s):
                copy.wait_send()

    for s in order:
        local(s).wait()

        def body(k, carry, s=s):
            send(lax.rem(me + k, peers), s).wait_send()
            return carry

        lax.fori_loop(1, peers, body, 0)

        def body(peer, carry, s=s):
            for j in range(1, gyn):
                passed(peer, s, j).wait()
            return carry

        lax.fori_loop(0, peers, body, 0)


def correlate_kernel(gyn, times, rows_per, rows_kept, inverse, g_ref, out_ref, wide, right, turned_ref):
    x = lax.axis_index("gy")
    c = pl.program_id(0)
    inputs = g_ref.shape[2]
    depth = right.shape[1]

    @pl.when(c == 0)
    def _():
        right[...] = jnp.zeros_like(right)
        for y in range(gyn):
            def body(t, carry, y=y):
                source = pl.ds(pl.multiple_of(t * rows_per, rows_per), rows_per)
                target = pl.ds(pl.multiple_of(t * rows_kept, rows_kept), rows_kept)
                block = g_ref[y, source, :].astype(F32)[:rows_kept]
                for lane in range(inputs // LANES):
                    wide[y, lane, target, :] = block[:, lane * LANES : (lane + 1) * LANES]
                return carry

            lax.fori_loop(0, times, body, 0)

    def prepare(h):
        def part(y, r):
            rows = pl.ds(2 * (PER * c + h) + r, times, rows_kept)
            return jnp.concatenate(
                [wide[y, lane, rows, :] for lane in range(inputs // LANES)], axis=1
            )

        for y in range(gyn):
            columns = slice(y * inputs, (y + 1) * inputs)
            right[h, 0:times, columns] = part(y, 0).astype(BF16)
            right[h, times : 2 * times, columns] = part(y, 1).astype(BF16)

        real, imag = part(x, 0), part(x, 1)
        rest = [jnp.zeros((depth - 2 * times, inputs), F32)] if depth > 2 * times else []
        for r, pieces in enumerate(([real, imag], [imag, -real])):
            turned = jnp.transpose(jnp.concatenate(pieces + rest, axis=0))
            turned_ref[h, r * inputs : (r + 1) * inputs, :] = turned.astype(BF16)

    def multiply(h):
        wide_n = min(NB, inputs)
        for col in range(0, gyn * inputs, wide_n):
            columns = slice(col, col + wide_n)
            product = jnp.dot(turned_ref[h], right[h, :, columns], preferred_element_type=F32)
            product = (product * inverse).astype(BF16)
            for r in range(2):
                out_ref[h, r, :, columns] = product[r * inputs : (r + 1) * inputs]

    for h in range(PER):
        prepare(h)
    for h in range(PER):
        multiply(h)


def solution(mesh):
    gxn, gzn, gyn = mesh.shape["gx"], mesh.shape["gz"], mesh.shape["gy"]
    peers = gxn * gzn
    chans = CHANS // peers
    rows_per = -(-2 * chans // 16) * 16
    rows_kept = -(-2 * chans // 8) * 8
    taps = filter_taps()
    basis = basis_rows(peers, rows_per)

    def spread(voltages):
        inputs = voltages.shape[0]
        spec = voltages.shape[1] // POINTS
        times = spec * peers
        dma = pltpu.SemaphoreType.DMA
        return pl.pallas_call(
            functools.partial(spread_kernel, gxn, gzn, gyn, spec, rows_per),
            out_shape=jax.ShapeDtypeStruct((gyn, times * rows_per, inputs), BF16),
            in_specs=[pl.BlockSpec(memory_space=pl.ANY)] * 3,
            out_specs=pl.BlockSpec(memory_space=pltpu.VMEM),
            scratch_shapes=[
                pltpu.VMEM(voltages.shape, jnp.int32),
                pltpu.VMEM(taps.shape, F32),
                pltpu.VMEM(basis.shape, BF16),
                pltpu.VMEM((spec + TAPS - 1, inputs, POINTS), BF16),
                pltpu.VMEM((spec, peers * rows_per, inputs), BF16),
                pltpu.VMEM((TAPS - 1, peers * rows_per, inputs), BF16),
                pltpu.VMEM((TAPS - 1, peers * rows_per, inputs), BF16),
                dma((LOADS + 2,)),
                dma((peers, spec)),
                dma((peers, spec)),
                dma((gyn - 1, peers, spec)),
                dma((gyn - 1, peers, spec)),
                dma((spec,)),
                dma((2, TAPS - 1, CUTS)),
            ],
            compiler_params=pltpu.CompilerParams(
                collective_id=0, has_side_effects=True, vmem_limit_bytes=60 * 2**20
            ),
        )(voltages, jnp.asarray(taps), jnp.asarray(basis, BF16))

    def correlate(gathered):
        inputs, times = gathered.shape[2], gathered.shape[1] // rows_per
        depth = -(-2 * times // 128) * 128
        return pl.pallas_call(
            functools.partial(
                correlate_kernel, gyn, times, rows_per, rows_kept, 1.0 / times
            ),
            grid=(chans // PER,),
            out_shape=jax.ShapeDtypeStruct((chans, 2, inputs, gyn * inputs), BF16),
            in_specs=[
                pl.BlockSpec(
                    (gyn, times * rows_per, inputs),
                    lambda c: (0, 0, 0),
                    pipeline_mode=pl.Buffered(1),
                )
            ],
            out_specs=pl.BlockSpec((PER, 2, inputs, gyn * inputs), lambda c: (c, 0, 0, 0)),
            scratch_shapes=[
                pltpu.VMEM((gyn, inputs // LANES, times * rows_kept, LANES), F32),
                pltpu.VMEM((PER, depth, gyn * inputs), BF16),
                pltpu.VMEM((PER, 2 * inputs, depth), BF16),
            ],
            compiler_params=pltpu.CompilerParams(
                dimension_semantics=("arbitrary",), vmem_limit_bytes=60 * 2**20
            ),
        )(gathered)

    def per_device(voltages):
        return correlate(spread(voltages))

    return jax.shard_map(
        per_device,
        mesh=mesh,
        in_specs=(P("gy", ("grp", "gx", "gz")),),
        out_specs=P(("grp", "gx", "gz"), None, "gy", None),
        check_vma=False,
    )
```
